256 devices in a mesh: member: 8 (over x, core), band: 32 (over z, y).
Axes of the slice: x: 4, y: 4, z: 8, core: 2. Of those that a mesh axis runs over, the one named last changes fastest.
Arguments:
- grid: float32 [384, 640, 1280], P('member', 'band'), parts along dimension 0, may hold values from -6 to 6
- row_points: int32 [640], replicated, may hold values from 20 to 1280, as said below
- row_latitude: int32 [640], replicated, may hold values from 0 to 639, as said below
- order_owner: int32 [320], replicated, may hold values from 0 to 31, as said below
- legendre: bfloat16 [640, 320, 320], P('band'), may hold values from -6 to 6
Outputs:
- spectral: float32 [640, 2, 384, 320], P('band', None, 'member'), parts along dimension 2
- energy: float32 [384, 320], P('member'), parts along dimension 0
The draws below stay inside these ranges and needn't reach their ends.
There are 8 independent parts, one for each index of `member`. The reference program is written for one: setup_inputs(seed, part) draws one part's arguments, and reference() takes and returns one part's arrays. A program takes and returns all parts, laid end to end along the dimension named above; an argument that names none is the same for every part. Nothing has to cross between parts.
Inputs may be any that keep to these rules, and one draw needn't show every extreme that they name: row_points is the same for a row and its mirror row 639-l, never falls from a pole towards the equator, is a multiple of 4, is 20 at the pole rows and equals 1280 at the equator rows. row_latitude is a permutation; the first 320 stored rows hold northern latitudes, and stored row 639-r holds the mirror 640 - 1-l of the latitude l of stored row r. order_owner never falls with the order; each device owns at most 20 orders, and one device owns exactly 20 in every draw.
All inputs are finite; a program needn't handle non-finite values.
Results may differ from the reference program's by a relative error of at most 0.0029.
Values may be sent and summed in bfloat16 or wider, within the bound.
A program may use at most 256 MiB of HBM per device.

```python
import math
import jax
import jax.numpy as jnp
from jax import lax

NN = 320
NLAT = 640
NLONMAX = 1280
F = 48
NLATH = 320
MCAP = 20
N_BAND = 32


def draw_row_points(key, part):
    key = jax.random.fold_in(key, 5)
    lat_index = jnp.arange(NLATH, dtype=jnp.int32)
    jitter = jax.random.randint(key, (NLATH,), -2, 3, dtype=jnp.int32)
    points = jnp.minimum(NLONMAX, 4 * (5 + lat_index + jitter))
    points = jnp.where(lat_index == 0, 20, points)
    points = jnp.where(lat_index == NLATH - 1, NLONMAX, points)
    points = lax.cummax(points, axis=0)
    return jnp.concatenate([points, points[::-1]]).astype(jnp.int32)


def draw_row_latitude(key, part):
    key = jax.random.fold_in(key, 7)
    half_bands = N_BAND // 2
    block_rows = NLAT // N_BAND
    block_order = jax.random.permutation(key, half_bands).astype(jnp.int32)
    stored = jnp.arange(NLATH, dtype=jnp.int32)
    northern = block_order[stored // block_rows] * block_rows + stored % block_rows
    southern = NLAT - 1 - northern[::-1]
    return jnp.concatenate([northern, southern]).astype(jnp.int32)


def draw_order_owner(key, part):
    key = jax.random.fold_in(key, 11)
    first_key, second_key = jax.random.split(key)
    heavy = jax.random.randint(first_key, (), 0, N_BAND, dtype=jnp.int32)
    remain = NN - MCAP
    base = remain // (N_BAND - 1)
    extra = remain % (N_BAND - 1)
    shuffled = jax.random.permutation(second_key, N_BAND - 1).astype(jnp.int32)
    others = base + (shuffled < extra).astype(jnp.int32)
    devices = jnp.arange(N_BAND, dtype=jnp.int32)
    position = jnp.clip(devices - (devices > heavy).astype(jnp.int32), 0, N_BAND - 2)
    counts = jnp.where(devices == heavy, MCAP, others[position])
    ends = jnp.cumsum(counts)
    orders = jnp.arange(NN, dtype=jnp.int32)
    owner = jnp.sum((ends[None, :] <= orders[:, None]).astype(jnp.int32), axis=1)
    return owner.astype(jnp.int32)


def block_levels(stream_key, dims, cuts, low, top_value):
    gain, own = 1.0, jax.random.fold_in(stream_key, 6)
    for axis_at, blocks in cuts:
        draws = jnp.exp(jax.random.uniform(jax.random.fold_in(own, axis_at), (blocks,), jnp.float32, low / len(cuts), top_value / len(cuts)))
        gain = gain * jnp.repeat(draws, dims[axis_at] // blocks).reshape([-1 if axis == axis_at else 1 for axis in range(len(dims))])
    return gain


def centred(key, dims, width, reach, pieces=(), held_as=jnp.bfloat16):
    values = width * jax.random.normal(key, dims, jnp.float32)
    if pieces:
        values = values * block_levels(key, dims, pieces, -0.22, 0.18)
    return jnp.clip(values, -reach, reach).astype(held_as)


def setup_inputs(seed: int = 0, part: int = 0) -> dict:
    streams_of = jax.random.split(jax.random.key(seed), 6)
    own_keys = jax.random.split(jax.random.fold_in(streams_of[5], part), 6)
    return {
        "grid": centred(own_keys[0], (F, NLAT, NLONMAX), 1.0, 6.0, ((1, 32),), jnp.float32),
        "row_points": draw_row_points(jax.random.fold_in(streams_of[5], 71), part),
        "row_latitude": draw_row_latitude(jax.random.fold_in(streams_of[5], 71), part),
        "order_owner": draw_order_owner(jax.random.fold_in(streams_of[5], 71), part),
        "legendre": centred(streams_of[4], (N_BAND * MCAP, NN, NLATH), 1.6, 6.0, ((0, 32),)),
    }


def fourier_row(row_values, length):
    columns = jnp.arange(NLONMAX, dtype=jnp.int32)
    orders = jnp.arange(NN, dtype=jnp.int32)
    phase = (orders[:, None] * columns[None, :]) % length
    length_real = length.astype(jnp.float32)
    angle = phase.astype(jnp.float32) * (2.0 * math.pi / length_real)
    keep = (columns[None, :] < length) & (orders[:, None] <= (length - 1) // 2)
    weight = jnp.where(keep, 1.0 / length_real, jnp.zeros((), jnp.float32))
    table = jnp.concatenate([jnp.cos(angle) * weight, -jnp.sin(angle) * weight], axis=0)
    result = lax.dot_general(table, row_values, (((1,), (1,)), ((), ())),
                             precision=lax.Precision.HIGHEST, preferred_element_type=jnp.float32)
    field_count = row_values.shape[0]
    return result.reshape(2, NN, field_count).transpose(1, 0, 2).reshape(NN, 2 * field_count)


def owned_orders(order_owner, owners, ranks):
    orders = jnp.arange(NN, dtype=jnp.int32)
    local = order_owner[None, :] == owners[:, None]
    position = jnp.cumsum(local.astype(jnp.int32), axis=1) - 1
    match = local & (position == ranks[:, None])
    slot_order = jnp.sum(jnp.where(match, orders[None, :], 0), axis=1).astype(jnp.int32)
    valid = jnp.any(match, axis=1)
    return slot_order, valid


def reference(grid, row_points, row_latitude, order_owner, legendre):
    field_count = grid.shape[0]
    lengths = jnp.take(row_points, row_latitude)

    def transform_pair(pair):
        return fourier_row(pair[0], pair[1])

    fourier = lax.map(transform_pair, (jnp.transpose(grid, (1, 0, 2)), lengths)).astype(jnp.bfloat16)
    slot_ids = jnp.arange(N_BAND * MCAP, dtype=jnp.int32)
    slot_order, valid = owned_orders(order_owner, slot_ids // MCAP, slot_ids % MCAP)
    column = jnp.where(row_latitude < NLATH, row_latitude, NLAT - 1 - row_latitude)
    southern = row_latitude >= NLATH
    degrees = jnp.arange(NN, dtype=jnp.int32)

    def per_slot(triple):
        table_slot, order, present = triple
        gathered = jnp.take(table_slot, column, axis=1)
        parity = jnp.where((degrees + order) % 2 == 0, 1.0, -1.0).astype(jnp.bfloat16)
        signed = jnp.where(southern[None, :], gathered * parity[:, None], gathered)
        order_rows = lax.dynamic_index_in_dim(fourier, order, axis=1, keepdims=False)
        coeffs = jnp.dot(signed, order_rows, preferred_element_type=jnp.float32)
        keep = (degrees >= order) & present
        coeffs = jnp.where(keep[:, None], coeffs, jnp.zeros((), jnp.float32))
        return coeffs.T.reshape(2, field_count, NN)

    spectral = lax.map(per_slot, (legendre, slot_order, valid))
    weight = jnp.where(valid, jnp.where(slot_order == 0, 1.0, 2.0), 0.0).astype(jnp.float32)
    power = jnp.einsum('scfn,s->fn', spectral * spectral, weight, precision=lax.Precision.HIGHEST)
    energy = power / (2 * degrees + 1).astype(jnp.float32)
    return spectral, energy
```

```python
import functools
import math

import jax
import jax.numpy as jnp
from jax import lax
from jax.experimental import pallas as pl
from jax.experimental.pallas import tpu as pltpu
from jax.sharding import PartitionSpec as P

NN = 320
F = 48
ROWS = 20
CAP = 20
BAND = 32
NLATH = 320
GROUPS = 4
LT = 248
VMEM = 56 * 1024 * 1024
MESH = pl.DeviceIdType.MESH


def cos_sin(turns):
    x = (turns - jnp.floor(turns + 0.5)) * (2.0 * math.pi)
    y = x * x
    c = jnp.full_like(x, 1.0 / math.factorial(20))
    for n in range(18, -2, -2):
        c = 1.0 / math.factorial(n) - c * y
    s = jnp.full_like(x, 1.0 / math.factorial(21))
    for n in range(19, -1, -2):
        s = 1.0 / math.factorial(n) - s * y
    return c, s * x


def cmul(a, b):
    return a[0] * b[0] - a[1] * b[1], a[0] * b[1] + a[1] * b[0]


def split(x):
    hi = x.astype(jnp.bfloat16)
    return hi, (x - hi.astype(jnp.float32)).astype(jnp.bfloat16)


def fourier_kernel(start_ref, lat_ref, points_ref, x_ref, out_ref, w_ref, bhi_ref, blo_ref, f_ref):
    r = pl.program_id(0)
    me = lax.axis_index("band")
    length = points_ref[lat_ref[me * ROWS + r]]
    quarter = length // 4
    f32 = jnp.float32

    @pl.when(r == 0)
    def _():
        f_ref[240 * 24 :, :] = jnp.zeros((8 * 24, 128), f32)
        zero = jnp.zeros((F, 384), jnp.bfloat16)
        for ref in (bhi_ref, blo_ref):
            ref[0:48, 384:768] = zero
            ref[48:96, 0:384] = zero

    qf = jnp.full((8, 128), quarter, jnp.int32).astype(f32)
    inv_q = 1.0 / qf
    inv_l = 0.25 * inv_q
    sub = lax.broadcasted_iota(jnp.int32, (8, 128), 0)
    lane = lax.broadcasted_iota(jnp.int32, (8, 128), 1)

    def turns_of(count):
        num = count.astype(f32)
        return (num - jnp.floor(num * inv_q) * qf) * inv_q

    table = cos_sin(turns_of(sub * lane))
    step = cos_sin(turns_of(8 * lane))
    tiles = [table]
    while len(tiles) < 48:
        room = 48 - len(tiles)
        tiles = tiles + [cmul(t, step) for t in tiles[:room]]
        step = cmul(step, step)
    for a in range(0, 48, 2):
        rows = 8 * a + lax.broadcasted_iota(jnp.int32, (16, 128), 0)
        scale = jnp.where(rows < quarter, jnp.concatenate([inv_l, inv_l], axis=0), 0.0)
        for part in range(2):
            value = jnp.concatenate([tiles[a][part], tiles[a + 1][part]], axis=0) * scale
            hi, lo = split(value)
            at = part * 384 + 8 * a
            w_ref[at : at + 16, 0:128] = hi
            w_ref[at : at + 16, 128:256] = lo

    psub = lax.broadcasted_iota(jnp.int32, (8, 384), 0)
    plane = lax.broadcasted_iota(jnp.int32, (8, 384), 1)
    lf = jnp.full((8, 384), length, jnp.int32).astype(f32)
    tc, ts = cos_sin((psub * plane).astype(f32) / lf)

    lane48 = lax.broadcasted_iota(jnp.int32, (F, 128), 1)

    def window(q):
        offset = q * quarter
        tile = offset >> 7
        rest = offset & 127
        parts = []
        for b in range(4):
            at = pl.multiple_of(jnp.minimum(tile + b, 9) * 128, 128)
            parts.append(pltpu.roll(x_ref[0, :, pl.ds(at, 128)], (128 - rest) & 127, axis=1))
        here = lane48 < 128 - rest
        return [jnp.where(here, parts[b], parts[b + 1]) for b in range(3)]

    w1, w2, w3 = window(1), window(2), window(3)
    for b in range(3):
        lo_at, hi_at = 128 * b, 128 * b + 128
        x0 = x_ref[0, :, lo_at:hi_at]
        e0, o0 = x0 + w2[b], x0 - w2[b]
        e1, o1 = w1[b] + w3[b], w1[b] - w3[b]
        c1, c2, c3 = (tc[p : p + 1, lo_at:hi_at] for p in (1, 2, 3))
        s1, s2, s3 = (ts[p : p + 1, lo_at:hi_at] for p in (1, 2, 3))
        y2 = e0 - e1
        pairs = [
            (e0 + e1, None),
            (o0 * c1 - o1 * s1, -(o0 * s1 + o1 * c1)),
            (y2 * c2, -(y2 * s2)),
            (o0 * c3 + o1 * s3, o1 * c3 - o0 * s3),
        ]
        for p, (zr, zi) in enumerate(pairs):
            top, mid = 96 * p, 96 * p + 48
            for ref, value in zip((bhi_ref, blo_ref), split(zr)):
                ref[top : top + 48, lo_at:hi_at] = value
                ref[mid : mid + 48, 384 + lo_at : 384 + hi_at] = -value
            if zi is not None:
                for ref, value in zip((bhi_ref, blo_ref), split(zi)):
                    ref[top : top + 48, 384 + lo_at : 384 + hi_at] = value
                    ref[mid : mid + 48, lo_at:hi_at] = value

    first = jnp.dot(bhi_ref[...], w_ref[...], preferred_element_type=f32)
    second = jnp.dot(blo_ref[...], w_ref[:, 0:128], preferred_element_type=f32)
    total = first[:, 0:128] + first[:, 128:256] + second
    for t in range(3):
        turned = total[128 * t : 128 * t + 128].T[:80]
        k = lax.broadcasted_iota(jnp.int32, (80, 128), 0)
        col = 128 * t + lax.broadcasted_iota(jnp.int32, (80, 128), 1)
        p = (col >= 96).astype(jnp.int32) + (col >= 192).astype(jnp.int32) + (col >= 288).astype(jnp.int32)
        kept = jnp.where(4 * k + p < length // 2, turned, 0.0)
        f_ref[pl.ds(t * 24 + r, 80, stride=72), :] = kept

    @pl.when(r == ROWS - 1)
    def _():
        lane24 = lax.broadcasted_iota(jnp.int32, (24, 128), 1)
        low = lax.broadcasted_iota(jnp.int32, (8, 128), 0) < 4

        def pack(d, carry):
            for g in range(GROUPS):
                order = jnp.minimum(start_ref[d] + 5 * g, NN)
                at = pl.multiple_of(((3 * order) >> 2) * 24, 8)
                rest = (96 * order) & 127
                rolled = pltpu.roll(f_ref[pl.ds(at, 120), :], (128 - rest) & 127, axis=1)
                here = lane24 < 128 - rest
                tails = []
                for j in range(4):
                    v = jnp.where(here, rolled[24 * j : 24 * j + 24], rolled[24 * j + 24 : 24 * j + 48])
                    out_ref[g, d, 16 * j : 16 * j + 16, :] = v[:16].astype(jnp.bfloat16)
                    tails.append(v[16:24])
                ext = jnp.concatenate(
                    [jnp.where(low, tails[j], pltpu.roll(tails[j + 1], 4, axis=0)) for j in (0, 2)], axis=0
                )
                out_ref[g, d, 64:80, :] = ext.astype(jnp.bfloat16)
            return carry

        lax.fori_loop(0, BAND, pack, 0)


def fourier(starts, row_latitude, row_points, rows):
    smem = pl.BlockSpec(memory_space=pltpu.SMEM)
    return pl.pallas_call(
        fourier_kernel,
        grid=(ROWS,),
        in_specs=[smem, smem, smem, pl.BlockSpec((1, F, 1280), lambda r: (r, 0, 0))],
        out_specs=pl.BlockSpec((GROUPS, BAND, 80, 128), lambda r: (0, 0, 0, 0)),
        out_shape=jax.ShapeDtypeStruct((GROUPS, BAND, 80, 128), jnp.bfloat16),
        scratch_shapes=[
            pltpu.VMEM((768, 256), jnp.bfloat16),
            pltpu.VMEM((384, 768), jnp.bfloat16),
            pltpu.VMEM((384, 768), jnp.bfloat16),
            pltpu.VMEM((LT * 24, 128), jnp.float32),
        ],
        compiler_params=pltpu.CompilerParams(vmem_limit_bytes=VMEM),
        name="fourier",
    )(starts, row_latitude, row_points, rows)


def exchange_kernel(start_ref, send_ref, leg_ref, pick_ref, spec_ref, energy_ref,
                    recv, lp, xt, power, pieces, parts, result, final,
                    send_sem, recv_sem, own_sem, power_send, power_recv, final_send, final_recv):
    me = lax.axis_index("band")
    f32 = jnp.float32
    barrier = pltpu.get_barrier_semaphore()

    def greet(o, carry):
        pl.semaphore_signal(barrier, inc=1, device_id={"band": lax.rem(me + o, BAND)}, device_id_type=MESH)
        return carry

    lax.fori_loop(1, BAND, greet, 0)
    own = [pltpu.make_async_copy(send_ref.at[g, me], recv.at[g, me], own_sem.at[g]) for g in range(GROUPS)]
    for copy in own:
        copy.start()
    pl.semaphore_wait(barrier, BAND - 1)

    for g in range(GROUPS):
        def send(o, carry, g=g):
            peer = lax.rem(me + o, BAND)
            pltpu.make_async_remote_copy(
                src_ref=send_ref.at[g, peer],
                dst_ref=recv.at[g, me],
                send_sem=send_sem.at[g],
                recv_sem=recv_sem.at[g],
                device_id={"band": peer},
                device_id_type=MESH,
            ).start()
            return carry

        lax.fori_loop(1, BAND, send, 0)

    start = start_ref[me]
    count = start_ref[me + 1] - start
    degree = lax.broadcasted_iota(jnp.int32, (1, NN), 1)

    def permute(s, carry):
        sign = (1 - 2 * ((degree + start + s) & 1)).astype(f32)
        value = lax.dot_general(
            pick_ref[...], leg_ref[s], (((1,), (1,)), ((), ())), preferred_element_type=f32
        )
        lp[s, 0:256, :] = value[0:256].astype(jnp.bfloat16)
        lp[s, 256:512, :] = (value[256:512] * sign).astype(jnp.bfloat16)
        lp[s, 512:576, :] = value[512:576].astype(jnp.bfloat16)
        lp[s, 576:640, :] = (value[576:640] * sign).astype(jnp.bfloat16)
        return carry

    lax.fori_loop(0, CAP, permute, 0)
    power[...] = jnp.zeros_like(power)
    low = lax.broadcasted_iota(jnp.int32, (16, 8, 128), 1) < 4

    for g in range(GROUPS):
        own[g].wait()
        everyone = recv.at[g, 0 : BAND - 1]
        pltpu.make_async_copy(everyone, everyone, recv_sem.at[g]).wait()
        tails = recv[g, :, 64:80, :].astype(f32).reshape(16, 2, 2, 8, 128)
        for a in range(4):
            main = recv[g, :, 16 * a : 16 * a + 16, :].reshape(512, 128)
            xt[128 * a : 128 * a + 128, 0:512] = main.T
            even, odd = tails[:, 0, a // 2], tails[:, 1, a // 2]
            if a % 2 == 0:
                tail = jnp.where(low, even, pltpu.roll(odd, 4, axis=1))
            else:
                tail = jnp.where(low, pltpu.roll(even, 4, axis=1), odd)
            xt[128 * a : 128 * a + 128, 512:640] = tail.reshape(128, 128).T.astype(jnp.bfloat16)
        for i in range(5):
            s = 5 * g + i
            order = start + s
            value = jnp.dot(xt[96 * i : 96 * i + 96, :], lp[s], preferred_element_type=f32)
            first = jnp.where(s < count, order, NN)
            value = jnp.where(degree >= first, value, 0.0)
            spec_ref[s] = value
            weight = jnp.where(order == 0, 1.0, 2.0).astype(f32)
            re, im = value[0:48], value[48:96]
            power[:, 0:NN] += weight * (re * re + im * im)

    for j in range(18):
        pieces[j] = power[8 * (j // 3) : 8 * (j // 3) + 8, 128 * (j % 3) : 128 * (j % 3) + 128]

    def spread(j, carry):
        @pl.when(j != me)
        def _():
            pltpu.make_async_remote_copy(
                src_ref=pieces.at[j], dst_ref=parts.at[me], send_sem=power_send, recv_sem=power_recv,
                device_id={"band": j}, device_id_type=MESH,
            ).start()
        return carry

    lax.fori_loop(0, 18, spread, 0)

    @pl.when(me < 18)
    def _():
        parts[me] = pieces[me]
        others = parts.at[0 : BAND - 1]
        pltpu.make_async_copy(others, others, power_recv).wait()
        column = 128 * lax.rem(me, 3) + lax.broadcasted_iota(jnp.int32, (8, 128), 1)
        value = jnp.sum(parts[...], axis=0) / (2 * column + 1).astype(f32)
        result[...] = value
        final[me] = value

        def share(o, carry):
            pltpu.make_async_remote_copy(
                src_ref=result, dst_ref=final.at[me], send_sem=final_send, recv_sem=final_recv,
                device_id={"band": lax.rem(me + o, BAND)}, device_id_type=MESH,
            ).start()
            return carry

        lax.fori_loop(1, BAND, share, 0)
        most = final.at[0:17]
        pltpu.make_async_copy(most, most, final_recv).wait()
        pltpu.make_async_copy(others, others, final_send).wait()
        sent = pieces.at[0:17]
        pltpu.make_async_copy(sent, sent, power_send).wait()

    @pl.when(me >= 18)
    def _():
        pltpu.make_async_copy(final, final, final_recv).wait()
        pltpu.make_async_copy(pieces, pieces, power_send).wait()

    for j in range(18):
        g, t = j // 3, j % 3
        width = 128 if t < 2 else 64
        energy_ref[8 * g : 8 * g + 8, 128 * t : 128 * t + width] = final[j][:, :width]

    for g in range(GROUPS):
        everyone = send_ref.at[g, 0 : BAND - 1]
        pltpu.make_async_copy(everyone, everyone, send_sem.at[g]).wait()


def exchange(starts, packed, legendre, pick):
    vmem = pl.BlockSpec(memory_space=pltpu.VMEM)
    return pl.pallas_call(
        exchange_kernel,
        in_specs=[pl.BlockSpec(memory_space=pltpu.SMEM), pl.BlockSpec(memory_space=pl.ANY), vmem, vmem],
        out_specs=[vmem, vmem],
        out_shape=[
            jax.ShapeDtypeStruct((CAP, 2 * F, NN), jnp.float32),
            jax.ShapeDtypeStruct((F, NN), jnp.float32),
        ],
        scratch_shapes=[
            pltpu.VMEM((GROUPS, BAND, 80, 128), jnp.bfloat16),
            pltpu.VMEM((CAP, 640, NN), jnp.bfloat16),
            pltpu.VMEM((512, 640), jnp.bfloat16),
            pltpu.VMEM((F, 384), jnp.float32),
            pltpu.VMEM((18, 8, 128), jnp.float32),
            pltpu.VMEM((BAND, 8, 128), jnp.float32),
            pltpu.VMEM((8, 128), jnp.float32),
            pltpu.VMEM((18, 8, 128), jnp.float32),
            pltpu.SemaphoreType.DMA((GROUPS,)),
            pltpu.SemaphoreType.DMA((GROUPS,)),
            pltpu.SemaphoreType.DMA((GROUPS,)),
            pltpu.SemaphoreType.DMA,
            pltpu.SemaphoreType.DMA,
            pltpu.SemaphoreType.DMA,
            pltpu.SemaphoreType.DMA,
        ],
        compiler_params=pltpu.CompilerParams(collective_id=0, has_side_effects=True, vmem_limit_bytes=VMEM),
        name="exchange",
    )(starts, packed, legendre, pick)


def on_device(grid, row_points, row_latitude, order_owner, legendre):
    bands = jnp.arange(BAND + 1, dtype=jnp.int32)
    starts = jnp.sum((order_owner[None, :] < bands[:, None]).astype(jnp.int32), axis=1)
    by_device = row_latitude.reshape(BAND, ROWS)
    stacked = jnp.concatenate([by_device[:, :16].reshape(-1), by_device[:, 16:].reshape(-1)])
    column = jnp.where(stacked < NLATH, stacked, 2 * NLATH - 1 - stacked)
    pick = (column[:, None] == jnp.arange(NLATH, dtype=jnp.int32)[None, :]).astype(jnp.bfloat16)
    packed = fourier(starts, row_latitude, row_points, jnp.transpose(grid, (1, 0, 2)))
    spectral, energy = exchange(starts, packed, legendre, pick)
    return spectral.reshape(CAP, 2, F, NN), energy


def solution(mesh):
    in_specs = (P("member", "band", None), P(), P(), P(), P("band", None, None))
    out_specs = (P("band", None, "member", None), P("member", None))
    return jax.shard_map(
        on_device, mesh=mesh, in_specs=in_specs, out_specs=out_specs, check_vma=False
    )
```

```python
import functools
import math

import jax
import jax.numpy as jnp
from jax import lax
from jax.experimental import pallas as pl
from jax.experimental.pallas import tpu as pltpu
from jax.sharding import PartitionSpec as P

NN = 320
F = 48
ROWS = 20
CAP = 20
BAND = 32
NLATH = 320
SHORT = 10
LT = 248
VMEM = 56 * 1024 * 1024
MESH = pl.DeviceIdType.MESH
F32 = jnp.float32
BF16 = jnp.bfloat16


def cos_sin(turns):
    x = (turns - jnp.floor(turns + 0.5)) * (2.0 * math.pi)
    y = x * x
    c = jnp.full_like(x, 1.0 / math.factorial(20))
    for n in range(18, -2, -2):
        c = 1.0 / math.factorial(n) - c * y
    s = jnp.full_like(x, 1.0 / math.factorial(21))
    for n in range(19, -1, -2):
        s = 1.0 / math.factorial(n) - s * y
    return c, s * x


def cmul(a, b):
    return a[0] * b[0] - a[1] * b[1], a[0] * b[1] + a[1] * b[0]


def split(x):
    hi = x.astype(BF16)
    return hi, (x - hi.astype(F32)).astype(BF16)


def dft_row(x_ref, tile_ref, r, length, w_ref, bhi_ref, blo_ref, f_ref, slot):
    quarter = length // 4
    for t in range(10):
        tile_ref[t] = x_ref[r, :, 128 * t : 128 * t + 128]

    qf = jnp.full((8, 128), quarter, jnp.int32).astype(F32)
    inv_q = 1.0 / qf
    inv_l = 0.25 * inv_q
    sub = lax.broadcasted_iota(jnp.int32, (8, 128), 0)
    lane = lax.broadcasted_iota(jnp.int32, (8, 128), 1)

    def turns_of(count):
        num = count.astype(F32)
        return (num - jnp.floor(num * inv_q) * qf) * inv_q

    step = cos_sin(turns_of(8 * lane))
    tiles = [cos_sin(turns_of(sub * lane))]
    while len(tiles) < 48:
        room = 48 - len(tiles)
        tiles = tiles + [cmul(t, step) for t in tiles[:room]]
        step = cmul(step, step)
    for a in range(0, 48, 2):
        rows = 8 * a + lax.broadcasted_iota(jnp.int32, (16, 128), 0)
        scale = jnp.where(rows < quarter, jnp.concatenate([inv_l, inv_l], axis=0), 0.0)
        for part in range(2):
            value = jnp.concatenate([tiles[a][part], tiles[a + 1][part]], axis=0) * scale
            hi, lo = split(value)
            at = part * 384 + 8 * a
            w_ref[at : at + 16, 0:128] = hi
            w_ref[at : at + 16, 128:256] = lo

    psub = lax.broadcasted_iota(jnp.int32, (8, 384), 0)
    plane = lax.broadcasted_iota(jnp.int32, (8, 384), 1)
    lf = jnp.full((8, 384), length, jnp.int32).astype(F32)
    tc, ts = cos_sin((psub * plane).astype(F32) / lf)

    lane48 = lax.broadcasted_iota(jnp.int32, (F, 128), 1)

    def window(q):
        offset = q * quarter
        tile = offset >> 7
        rest = offset & 127
        parts = []
        for b in range(4):
            parts.append(pltpu.roll(tile_ref[jnp.minimum(tile + b, 9)], (128 - rest) & 127, axis=1))
        here = lane48 < 128 - rest
        return [jnp.where(here, parts[b], parts[b + 1]) for b in range(3)]

    w1, w2, w3 = window(1), window(2), window(3)
    for b in range(3):
        lo_at, hi_at = 128 * b, 128 * b + 128
        x0 = x_ref[r, :, lo_at:hi_at]
        e0, o0 = x0 + w2[b], x0 - w2[b]
        e1, o1 = w1[b] + w3[b], w1[b] - w3[b]
        c1, c2, c3 = (tc[p : p + 1, lo_at:hi_at] for p in (1, 2, 3))
        s1, s2, s3 = (ts[p : p + 1, lo_at:hi_at] for p in (1, 2, 3))
        y2 = e0 - e1
        pairs = [
            (e0 + e1, None),
            (o0 * c1 - o1 * s1, -(o0 * s1 + o1 * c1)),
            (y2 * c2, -(y2 * s2)),
            (o0 * c3 + o1 * s3, o1 * c3 - o0 * s3),
        ]
        for p, (zr, zi) in enumerate(pairs):
            top, mid = 96 * p, 96 * p + 48
            for ref, value in zip((bhi_ref, blo_ref), split(zr)):
                ref[top : top + 48, lo_at:hi_at] = value
                ref[mid : mid + 48, 384 + lo_at : 384 + hi_at] = -value
            if zi is not None:
                for ref, value in zip((bhi_ref, blo_ref), split(zi)):
                    ref[top : top + 48, 384 + lo_at : 384 + hi_at] = value
                    ref[mid : mid + 48, lo_at:hi_at] = value

    first = jnp.dot(bhi_ref[...], w_ref[...], preferred_element_type=F32)
    second = jnp.dot(blo_ref[...], w_ref[:, 0:128], preferred_element_type=F32)
    total = first[:, 0:128] + first[:, 128:256] + second
    for t in range(3):
        turned = total[128 * t : 128 * t + 128].T[:80]
        k = lax.broadcasted_iota(jnp.int32, (80, 128), 0)
        col = 128 * t + lax.broadcasted_iota(jnp.int32, (80, 128), 1)
        p = sum((col >= 96 * q).astype(jnp.int32) for q in (1, 2, 3))
        kept = jnp.where(4 * k + p < length // 2, turned, 0.0)
        f_ref[pl.ds(t, 80, stride=3), slot, :] = kept


def take_orders(f_ref, order, height):
    order = jnp.minimum(order, NN)
    rest = (96 * order) & 127
    tiles = f_ref[pl.ds((3 * order) >> 2, 5)].reshape(5 * height, 128)
    rolled = pltpu.roll(tiles, (128 - rest) & 127, axis=1)
    here = lax.broadcasted_iota(jnp.int32, (height, 128), 1) < 128 - rest
    cut = [rolled[height * j : height * (j + 1)] for j in range(5)]
    return [jnp.where(here, cut[j], cut[j + 1]) for j in range(4)]


def pack_a(f_ref, order):
    return jnp.concatenate(take_orders(f_ref, order, 8), axis=0).astype(BF16)


def pack_b(f_ref, order):
    v = take_orders(f_ref, order, 16)
    low = lax.broadcasted_iota(jnp.int32, (8, 128), 0) < 4
    tails = [jnp.where(low, v[j][8:], pltpu.roll(v[j + 1][8:], 4, axis=0)) for j in (0, 2)]
    return jnp.concatenate([v[j][:8] for j in range(4)] + tails, axis=0).astype(BF16)


def octets(block):
    wide = block.astype(F32).reshape(BAND, 4, 8, 128)
    return [wide[:, a].reshape(256, 128).T.astype(BF16) for a in range(4)]


def quads(block):
    wide = block.astype(F32).reshape(16, 2, 2, 8, 128)
    low = lax.broadcasted_iota(jnp.int32, (16, 8, 128), 1) < 4
    out = []
    for a in range(4):
        even, odd = wide[:, 0, a // 2], wide[:, 1, a // 2]
        if a % 2 == 0:
            tail = jnp.where(low, even, pltpu.roll(odd, 4, axis=1))
        else:
            tail = jnp.where(low, pltpu.roll(even, 4, axis=1), odd)
        out.append(tail.reshape(128, 128).T.astype(BF16))
    return out


def wait(ref, sem):
    pltpu.make_async_copy(ref, ref, sem).wait()


def fused_kernel(short, start_ref, lat_ref, points_ref, grid_ref, leg_hbm, pick_ref, spec_ref, energy_ref,
                 x_ref, tile_ref, leg_ref, w_ref, bhi_ref, blo_ref, fa_ref, fb_ref,
                 send_a, send_b, recv_a, recv_b, over_a, over_b,
                 lp, xt, spec, power, pieces, parts, result, final,
                 x_sem, leg_sem, spec_sem, sent_a, sent_b, got_a, got_b,
                 hop1_sent, hop1_got, hop2_sent, hop2_got,
                 power_send, power_recv, final_send, final_recv):
    groups = 2 if short else 4
    me = lax.axis_index("band")
    z, y = me // 4, lax.rem(me, 4)
    barrier = pltpu.get_barrier_semaphore()

    def greet(o, carry):
        pl.semaphore_signal(barrier, inc=1, device_id={"band": lax.rem(me + o, BAND)}, device_id_type=MESH)
        return carry

    def load(r):
        return pltpu.make_async_copy(grid_ref.at[r], x_ref.at[r], x_sem.at[r])

    def load_row(r, carry):
        load(r).start()
        return carry

    lax.fori_loop(0, ROWS, load_row, 0)
    lax.fori_loop(1, BAND, greet, 0)
    leg_copy = pltpu.make_async_copy(leg_hbm, leg_ref, leg_sem)
    leg_copy.start()

    fa_ref[240:] = jnp.zeros((8, 8, 128), F32)
    fb_ref[240:] = jnp.zeros((8, 16, 128), F32)
    zero = jnp.zeros((F, 384), BF16)
    for ref in (bhi_ref, blo_ref):
        ref[0:48, 384:768] = zero
        ref[48:96, 0:384] = zero

    def dft(first, f_ref):
        def body(r, carry):
            load(r).wait()
            length = points_ref[lat_ref[me * ROWS + r]]
            dft_row(x_ref, tile_ref, r, length, w_ref, bhi_ref, blo_ref, f_ref, r - first)
            return carry
        return body

    def pack_all(packer, f_ref, send, recv, over):
        def body(d, carry):
            for g in range(groups):
                send[g, d] = packer(f_ref, start_ref[d] + 5 * g)
            return carry
        lax.fori_loop(0, BAND, body, 0)
        for g in range(groups):
            recv[g, me] = send[g, me]
        if short:
            for j in range(2):
                over[z, y, j] = packer(f_ref, start_ref[BAND + 1] + 5 * j)

    def send_all(c, send, recv, over, sent, got):
        if short:
            def hop1(o, carry):
                pltpu.make_async_remote_copy(
                    src_ref=over.at[z, y], dst_ref=over.at[z, y],
                    send_sem=hop1_sent.at[c], recv_sem=hop1_got.at[c],
                    device_id={"band": lax.rem(z + o, 8) * 4 + y}, device_id_type=MESH,
                ).start()
                return carry
            lax.fori_loop(1, 8, hop1, 0)
        for g in range(groups):
            def body(o, carry, g=g):
                peer = lax.rem(me + o, BAND)
                pltpu.make_async_remote_copy(
                    src_ref=send.at[g, peer], dst_ref=recv.at[g, me],
                    send_sem=sent.at[g], recv_sem=got.at[g],
                    device_id={"band": peer}, device_id_type=MESH,
                ).start()
                return carry
            lax.fori_loop(1, BAND, body, 0)

    def forward(c, over):
        wait(over.at[0:7, 0], hop1_got.at[c])
        def hop2(o, carry):
            pltpu.make_async_remote_copy(
                src_ref=over.at[:, y], dst_ref=over.at[:, y],
                send_sem=hop2_sent.at[c], recv_sem=hop2_got.at[c],
                device_id={"band": z * 4 + lax.rem(y + o, 4)}, device_id_type=MESH,
            ).start()
            return carry
        lax.fori_loop(1, 4, hop2, 0)

    lax.fori_loop(0, 8, dft(0, fa_ref), 0)
    pack_all(pack_a, fa_ref, send_a, recv_a, over_a)
    pl.semaphore_wait(barrier, BAND - 1)
    send_all(0, send_a, recv_a, over_a, sent_a, got_a)
    lax.fori_loop(8, ROWS, dft(8, fb_ref), 0)
    pack_all(pack_b, fb_ref, send_b, recv_b, over_b)
    send_all(1, send_b, recv_b, over_b, sent_b, got_b)
    leg_copy.wait()

    start = start_ref[me]
    count = start_ref[me + 1] - start
    degree = lax.broadcasted_iota(jnp.int32, (1, NN), 1)

    def permute(s, carry):
        sign = (1 - 2 * ((degree + start + s) & 1)).astype(F32)
        value = lax.dot_general(
            pick_ref[...], leg_ref[s], (((1,), (1,)), ((), ())), preferred_element_type=F32
        )
        for at, size, south in ((0, 128, 0), (128, 128, 1), (256, 128, 0), (384, 128, 1), (512, 64, 0), (576, 64, 1)):
            piece = value[at : at + size]
            lp[s, at : at + size, :] = (piece * sign if south else piece).astype(BF16)
        return carry

    lax.fori_loop(0, SHORT, permute, 0)
    if short:
        forward(0, over_a)
    lax.fori_loop(SHORT, CAP, permute, 0)
    if short:
        forward(1, over_b)
    power[...] = jnp.zeros_like(power)

    for g in range(4):
        if g < groups:
            wait(recv_a.at[g, 0 : BAND - 1], got_a.at[g])
            block_a = recv_a[g]
        else:
            if g == groups:
                wait(over_a.at[:, 0:3], hop2_got.at[0])
            block_a = over_a[:, :, g - groups].reshape(BAND, 32, 128)
        for a, value in enumerate(octets(block_a)):
            xt[128 * a : 128 * a + 128, 0:256] = value
        if g < groups:
            wait(recv_b.at[g, 0 : BAND - 1], got_b.at[g])
            block_b = recv_b[g]
        else:
            if g == groups:
                wait(over_b.at[:, 0:3], hop2_got.at[1])
            block_b = over_b[:, :, g - groups].reshape(BAND, 48, 128)
        for a, value in enumerate(octets(block_b[:, 0:32])):
            xt[128 * a : 128 * a + 128, 256:512] = value
        for a, value in enumerate(quads(block_b[:, 32:48])):
            xt[128 * a : 128 * a + 128, 512:640] = value
        for i in range(5):
            s = 5 * g + i
            order = start + s
            value = jnp.dot(xt[96 * i : 96 * i + 96, :], lp[s], preferred_element_type=F32)
            first = jnp.where(s < count, order, NN)
            value = jnp.where(degree >= first, value, 0.0)
            spec[s] = value
            weight = jnp.where(order == 0, 1.0, 2.0).astype(F32)
            re, im = value[0:48], value[48:96]
            power[:, 0:NN] += weight * (re * re + im * im)
        pltpu.make_async_copy(spec.at[5 * g : 5 * g + 5], spec_ref.at[5 * g : 5 * g + 5], spec_sem.at[g]).start()

    for j in range(18):
        pieces[j] = power[8 * (j // 3) : 8 * (j // 3) + 8, 128 * (j % 3) : 128 * (j % 3) + 128]

    def spread(j, carry):
        @pl.when(j != me)
        def _():
            pltpu.make_async_remote_copy(
                src_ref=pieces.at[j], dst_ref=parts.at[me], send_sem=power_send, recv_sem=power_recv,
                device_id={"band": j}, device_id_type=MESH,
            ).start()
        return carry

    lax.fori_loop(0, 18, spread, 0)

    @pl.when(me < 18)
    def _():
        parts[me] = pieces[me]
        others = parts.at[0 : BAND - 1]
        wait(others, power_recv)
        column = 128 * lax.rem(me, 3) + lax.broadcasted_iota(jnp.int32, (8, 128), 1)
        value = jnp.sum(parts[...], axis=0) / (2 * column + 1).astype(F32)
        result[...] = value
        final[me] = value

        def share(o, carry):
            pltpu.make_async_remote_copy(
                src_ref=result, dst_ref=final.at[me], send_sem=final_send, recv_sem=final_recv,
                device_id={"band": lax.rem(me + o, BAND)}, device_id_type=MESH,
            ).start()
            return carry

        lax.fori_loop(1, BAND, share, 0)
        wait(final.at[0:17], final_recv)
        wait(others, final_send)
        wait(pieces.at[0:17], power_send)

    @pl.when(me >= 18)
    def _():
        wait(final, final_recv)
        wait(pieces, power_send)

    for j in range(18):
        g, t = j // 3, j % 3
        width = 128 if t < 2 else 64
        energy_ref[8 * g : 8 * g + 8, 128 * t : 128 * t + width] = final[j][:, :width]

    for g in range(groups):
        wait(send_a.at[g, 0 : BAND - 1], sent_a.at[g])
        wait(send_b.at[g, 0 : BAND - 1], sent_b.at[g])
    if short:
        for c, over in ((0, over_a), (1, over_b)):
            wait(over.at[0:7, 0], hop1_sent.at[c])
            wait(over.at[:, 0:3], hop2_sent.at[c])
    for g in range(4):
        pltpu.make_async_copy(spec.at[5 * g : 5 * g + 5], spec_ref.at[5 * g : 5 * g + 5], spec_sem.at[g]).wait()


def fused(short, starts, row_latitude, row_points, rows, legendre, pick):
    groups = 2 if short else 4
    smem = pl.BlockSpec(memory_space=pltpu.SMEM)
    vmem = pl.BlockSpec(memory_space=pltpu.VMEM)
    hbm = pl.BlockSpec(memory_space=pl.ANY)
    dma = pltpu.SemaphoreType.DMA
    return pl.pallas_call(
        functools.partial(fused_kernel, short),
        in_specs=[smem, smem, smem, hbm, hbm, vmem],
        out_specs=[hbm, vmem],
        out_shape=[
            jax.ShapeDtypeStruct((CAP, 2 * F, NN), F32),
            jax.ShapeDtypeStruct((F, NN), F32),
        ],
        scratch_shapes=[
            pltpu.VMEM((ROWS, F, 1280), F32),
            pltpu.VMEM((10, F, 128), F32),
            pltpu.VMEM((CAP, NN, NLATH), BF16),
            pltpu.VMEM((768, 256), BF16),
            pltpu.VMEM((384, 768), BF16),
            pltpu.VMEM((384, 768), BF16),
            pltpu.VMEM((LT, 8, 128), F32),
            pltpu.VMEM((LT, 16, 128), F32),
            pltpu.VMEM((groups, BAND, 32, 128), BF16),
            pltpu.VMEM((groups, BAND, 48, 128), BF16),
            pltpu.VMEM((groups, BAND, 32, 128), BF16),
            pltpu.VMEM((groups, BAND, 48, 128), BF16),
            pltpu.VMEM((8, 4, 2, 32, 128), BF16),
            pltpu.VMEM((8, 4, 2, 48, 128), BF16),
            pltpu.VMEM((CAP, 640, NN), BF16),
            pltpu.VMEM((512, 640), BF16),
            pltpu.VMEM((CAP, 2 * F, NN), F32),
            pltpu.VMEM((F, 384), F32),
            pltpu.VMEM((18, 8, 128), F32),
            pltpu.VMEM((BAND, 8, 128), F32),
            pltpu.VMEM((8, 128), F32),
            pltpu.VMEM((18, 8, 128), F32),
            dma((ROWS,)), dma, dma((4,)),
            dma((groups,)), dma((groups,)), dma((groups,)), dma((groups,)),
            dma((2,)), dma((2,)), dma((2,)), dma((2,)),
            dma, dma, dma, dma,
        ],
        compiler_params=pltpu.CompilerParams(
            collective_id=0 if short else 1, has_side_effects=True, vmem_limit_bytes=VMEM
        ),
        name="short" if short else "full",
    )(starts, row_latitude, row_points, rows, legendre, pick)


def on_device(grid, row_points, row_latitude, order_owner, legendre):
    bands = jnp.arange(BAND + 1, dtype=jnp.int32)
    starts = jnp.sum((order_owner[None, :] < bands[:, None]).astype(jnp.int32), axis=1)
    crowded = starts[1:] - starts[:-1] > SHORT
    over = jnp.max(jnp.where(crowded, starts[:-1] + SHORT, 0))
    few = jnp.sum(crowded.astype(jnp.int32)) <= 1
    starts = jnp.concatenate([starts, over[None]])
    by_device = row_latitude.reshape(BAND, ROWS)
    stacked = jnp.concatenate([by_device[:, a:b].reshape(-1) for a, b in ((0, 8), (8, 16), (16, 20))])
    column = jnp.where(stacked < NLATH, stacked, 2 * NLATH - 1 - stacked)
    pick = (column[:, None] == jnp.arange(NLATH, dtype=jnp.int32)[None, :]).astype(BF16)
    rows = jnp.transpose(grid, (1, 0, 2))
    spectral, energy = lax.cond(
        few, functools.partial(fused, True), functools.partial(fused, False),
        starts, row_latitude, row_points, rows, legendre, pick,
    )
    return spectral.reshape(CAP, 2, F, NN), energy


def solution(mesh):
    in_specs = (P("member", "band", None), P(), P(), P(), P("band", None, None))
    out_specs = (P("band", None, "member", None), P("member", None))
    return jax.shard_map(
        on_device, mesh=mesh, in_specs=in_specs, out_specs=out_specs, check_vma=False
    )
```

```python
import functools
import math

import jax
import jax.numpy as jnp
from jax import lax
from jax.experimental import pallas as pl
from jax.experimental.pallas import tpu as pltpu
from jax.sharding import PartitionSpec as P

NN = 320
F = 48
ROWS = 20
CAP = 20
BAND = 32
NLATH = 320
SHORT = 10
LT = 248
VMEM = 56 * 1024 * 1024
MESH = pl.DeviceIdType.MESH
F32 = jnp.float32
BF16 = jnp.bfloat16


def cos_sin(turns):
    x = (turns - jnp.floor(turns + 0.5)) * (2.0 * math.pi)
    y = x * x
    c = jnp.full_like(x, 1.0 / math.factorial(20))
    for n in range(18, -2, -2):
        c = 1.0 / math.factorial(n) - c * y
    s = jnp.full_like(x, 1.0 / math.factorial(21))
    for n in range(19, -1, -2):
        s = 1.0 / math.factorial(n) - s * y
    return c, s * x


def cmul(a, b):
    return a[0] * b[0] - a[1] * b[1], a[0] * b[1] + a[1] * b[0]


def split(x):
    hi = x.astype(BF16)
    return hi, (x - hi.astype(F32)).astype(BF16)


def dft_row(x_ref, tile_ref, r, length, w_ref, bhi_ref, blo_ref, f_ref, slot):
    quarter = length // 4
    for t in range(10):
        tile_ref[t] = x_ref[r, :, 128 * t : 128 * t + 128]

    qf = jnp.full((8, 128), quarter, jnp.int32).astype(F32)
    inv_q = 1.0 / qf
    inv_l = 0.25 * inv_q
    sub = lax.broadcasted_iota(jnp.int32, (8, 128), 0)
    lane = lax.broadcasted_iota(jnp.int32, (8, 128), 1)

    def turns_of(count):
        num = count.astype(F32)
        return (num - jnp.floor(num * inv_q) * qf) * inv_q

    step = cos_sin(turns_of(8 * lane))
    tiles = [cos_sin(turns_of(sub * lane))]
    while len(tiles) < 48:
        room = 48 - len(tiles)
        tiles = tiles + [cmul(t, step) for t in tiles[:room]]
        step = cmul(step, step)
    for a in range(0, 48, 2):
        rows = 8 * a + lax.broadcasted_iota(jnp.int32, (16, 128), 0)
        scale = jnp.where(rows < quarter, jnp.concatenate([inv_l, inv_l], axis=0), 0.0)
        for part in range(2):
            value = jnp.concatenate([tiles[a][part], tiles[a + 1][part]], axis=0) * scale
            hi, lo = split(value)
            at = part * 384 + 8 * a
            w_ref[at : at + 16, 0:128] = hi
            w_ref[at : at + 16, 128:256] = lo

    psub = lax.broadcasted_iota(jnp.int32, (8, 384), 0)
    plane = lax.broadcasted_iota(jnp.int32, (8, 384), 1)
    lf = jnp.full((8, 384), length, jnp.int32).astype(F32)
    tc, ts = cos_sin((psub * plane).astype(F32) / lf)

    lane48 = lax.broadcasted_iota(jnp.int32, (F, 128), 1)

    def window(q):
        offset = q * quarter
        tile = offset >> 7
        rest = offset & 127
        parts = []
        for b in range(4):
            parts.append(pltpu.roll(tile_ref[jnp.minimum(tile + b, 9)], (128 - rest) & 127, axis=1))
        here = lane48 < 128 - rest
        return [jnp.where(here, parts[b], parts[b + 1]) for b in range(3)]

    w1, w2, w3 = window(1), window(2), window(3)
    for b in range(3):
        lo_at, hi_at = 128 * b, 128 * b + 128
        x0 = x_ref[r, :, lo_at:hi_at]
        e0, o0 = x0 + w2[b], x0 - w2[b]
        e1, o1 = w1[b] + w3[b], w1[b] - w3[b]
        c1, c2, c3 = (tc[p : p + 1, lo_at:hi_at] for p in (1, 2, 3))
        s1, s2, s3 = (ts[p : p + 1, lo_at:hi_at] for p in (1, 2, 3))
        y2 = e0 - e1
        pairs = [
            (e0 + e1, None),
            (o0 * c1 - o1 * s1, -(o0 * s1 + o1 * c1)),
            (y2 * c2, -(y2 * s2)),
            (o0 * c3 + o1 * s3, o1 * c3 - o0 * s3),
        ]
        for p, (zr, zi) in enumerate(pairs):
            top, mid = 96 * p, 96 * p + 48
            for ref, value in zip((bhi_ref, blo_ref), split(zr)):
                ref[top : top + 48, lo_at:hi_at] = value
                ref[mid : mid + 48, 384 + lo_at : 384 + hi_at] = -value
            if zi is not None:
                for ref, value in zip((bhi_ref, blo_ref), split(zi)):
                    ref[top : top + 48, 384 + lo_at : 384 + hi_at] = value
                    ref[mid : mid + 48, lo_at:hi_at] = value

    first = jnp.dot(bhi_ref[...], w_ref[...], preferred_element_type=F32)
    second = jnp.dot(blo_ref[...], w_ref[:, 0:128], preferred_element_type=F32)
    total = first[:, 0:128] + first[:, 128:256] + second
    for t in range(3):
        turned = total[128 * t : 128 * t + 128].T[:80]
        k = lax.broadcasted_iota(jnp.int32, (80, 128), 0)
        col = 128 * t + lax.broadcasted_iota(jnp.int32, (80, 128), 1)
        p = sum((col >= 96 * q).astype(jnp.int32) for q in (1, 2, 3))
        kept = jnp.where(4 * k + p < length // 2, turned, 0.0)
        f_ref[pl.ds(t, 80, stride=3), slot, :] = kept


def take_orders(f_ref, order):
    order = jnp.minimum(order, NN)
    rest = (96 * order) & 127
    tiles = f_ref[pl.ds((3 * order) >> 2, 5)].reshape(40, 128)
    rolled = pltpu.roll(tiles, (128 - rest) & 127, axis=1)
    here = lax.broadcasted_iota(jnp.int32, (8, 128), 1) < 128 - rest
    cut = [rolled[8 * j : 8 * j + 8] for j in range(5)]
    return [jnp.where(here, cut[j], cut[j + 1]) for j in range(4)]


def pack_eight(f_ref, order):
    return jnp.concatenate(take_orders(f_ref, order), axis=0).astype(BF16)


def pack_four(f_ref, order):
    v = take_orders(f_ref, order)
    low = lax.broadcasted_iota(jnp.int32, (8, 128), 0) < 4
    return jnp.concatenate(
        [jnp.where(low, v[j], pltpu.roll(v[j + 1], 4, axis=0)) for j in (0, 2)], axis=0
    ).astype(BF16)


def octets(block):
    wide = block.astype(F32).reshape(16, 4, 8, 128)
    return [wide[:, a].reshape(128, 128).T.astype(BF16) for a in range(4)]


def quads(block):
    wide = block.astype(F32).reshape(8, 2, 2, 8, 128)
    low = lax.broadcasted_iota(jnp.int32, (8, 8, 128), 1) < 4
    out = []
    for a in range(4):
        even, odd = wide[:, 0, a // 2], wide[:, 1, a // 2]
        if a % 2 == 0:
            tail = jnp.where(low, even, pltpu.roll(odd, 4, axis=1))
        else:
            tail = jnp.where(low, pltpu.roll(even, 4, axis=1), odd)
        out.append(tail.reshape(64, 128).T.astype(BF16))
    return out


def wait(ref, sem):
    pltpu.make_async_copy(ref, ref, sem).wait()


def far_first(i):
    a, b = i // 4, lax.rem(i, 4)
    dz = jnp.where(lax.rem(a, 2) == 1, 4 - (a + 1) // 2, 4 + a // 2)
    dy = jnp.where(lax.rem(b, 2) == 1, 2 - (b + 1) // 2, 2 + b // 2)
    return dz, dy


CHUNKS = ((0, 4, 256), (4, 8, 0), (12, 8, 128))


def fused_kernel(short, start_ref, lat_ref, points_ref, grid_ref, leg_hbm, pick_ref, spec_ref, energy_ref,
                 x_ref, tile_ref, leg_ref, w_ref, bhi_ref, blo_ref, f_ref,
                 send_0, send_1, send_2, recv_0, recv_1, recv_2, over_0, over_1, over_2,
                 lp, xt_n, xt_s, spec, power, pieces, parts, result, final,
                 x_sem, leg_sem, spec_sem, sent, got,
                 hop1_sent, hop1_got, hop2_sent, hop2_got,
                 power_send, power_recv, final_send, final_recv):
    groups = 2 if short else 4
    send, recv, over = (send_0, send_1, send_2), (recv_0, recv_1, recv_2), (over_0, over_1, over_2)
    me = lax.axis_index("band")
    z, y = me // 4, lax.rem(me, 4)
    place = jnp.where(me < 16, me, 47 - me)
    barrier = pltpu.get_barrier_semaphore()

    def greet(o, carry):
        pl.semaphore_signal(barrier, inc=1, device_id={"band": lax.rem(me + o, BAND)}, device_id_type=MESH)
        return carry

    def peer_of(i):
        dz, dy = far_first(i)
        return lax.rem(z + dz, 8) * 4 + lax.rem(y + dy, 4)

    def stored(r):
        return jnp.where(me < 16, r, ROWS - 1 - r)

    def load(r):
        return pltpu.make_async_copy(grid_ref.at[stored(r)], x_ref.at[r], x_sem.at[r])

    def load_row(r, carry):
        load(r).start()
        return carry

    lax.fori_loop(0, ROWS, load_row, 0)
    lax.fori_loop(1, BAND, greet, 0)
    leg_copy = pltpu.make_async_copy(leg_hbm, leg_ref, leg_sem)
    leg_copy.start()

    f_ref[240:] = jnp.zeros((8, 8, 128), F32)
    zero = jnp.zeros((F, 384), BF16)
    for ref in (bhi_ref, blo_ref):
        ref[0:48, 384:768] = zero
        ref[48:96, 0:384] = zero

    def crowd(d, carry):
        first = start_ref[d]
        return carry + jnp.where(start_ref[d + 1] - first > SHORT, first + SHORT, 0)

    extra = lax.fori_loop(0, BAND, crowd, 0) if short else None

    def dft_chunk(c):
        first, rows, _ = CHUNKS[c]

        def body(r, carry):
            load(r).wait()
            length = points_ref[lat_ref[me * ROWS + stored(r)]]
            dft_row(x_ref, tile_ref, r, length, w_ref, bhi_ref, blo_ref, f_ref, r - first)
            return carry

        lax.fori_loop(first, first + rows, body, 0)
        packer = pack_four if rows == 4 else pack_eight
        if short:
            for j in range(2):
                over[c][z, y, j] = packer(f_ref, extra + 5 * j)

        def pack(d, carry):
            for g in range(groups):
                send[c][d, g] = packer(f_ref, start_ref[d] + 5 * g)
            return carry

        lax.fori_loop(0, BAND, pack, 0, unroll=4)
        recv[c][place] = send[c][me]

    def send_chunk(c):
        if short:
            def hop1(o, carry):
                pltpu.make_async_remote_copy(
                    src_ref=over[c].at[z, y], dst_ref=over[c].at[z, y],
                    send_sem=hop1_sent.at[c], recv_sem=hop1_got.at[c],
                    device_id={"band": lax.rem(z + o, 8) * 4 + y}, device_id_type=MESH,
                ).start()
                return carry
            lax.fori_loop(1, 8, hop1, 0)

        def body(i, carry):
            peer = peer_of(i)
            pltpu.make_async_remote_copy(
                src_ref=send[c].at[peer], dst_ref=recv[c].at[place],
                send_sem=sent.at[c], recv_sem=got.at[c],
                device_id={"band": peer}, device_id_type=MESH,
            ).start()
            return carry

        lax.fori_loop(0, BAND - 1, body, 0)

    def forward(c):
        if not short:
            return
        wait(over[c].at[0:7, 0], hop1_got.at[c])

        def hop2(o, carry):
            pltpu.make_async_remote_copy(
                src_ref=over[c].at[:, y], dst_ref=over[c].at[:, y],
                send_sem=hop2_sent.at[c], recv_sem=hop2_got.at[c],
                device_id={"band": z * 4 + lax.rem(y + o, 4)}, device_id_type=MESH,
            ).start()
            return carry
        lax.fori_loop(1, 4, hop2, 0)

    dft_chunk(0)
    pl.semaphore_wait(barrier, BAND - 1)
    send_chunk(0)
    dft_chunk(1)
    send_chunk(1)
    forward(0)
    dft_chunk(2)
    send_chunk(2)
    leg_copy.wait()

    start = start_ref[me]
    count = start_ref[me + 1] - start
    degree = lax.broadcasted_iota(jnp.int32, (1, NN), 1)

    def permute(s, carry):
        lp[s] = lax.dot_general(
            pick_ref[...], leg_ref[s], (((1,), (1,)), ((), ())), preferred_element_type=F32
        ).astype(BF16)
        return carry

    lax.fori_loop(0, 2, permute, 0, unroll=2)
    forward(1)
    lax.fori_loop(2, SHORT, permute, 0, unroll=2)
    forward(2)
    lax.fori_loop(SHORT, CAP, permute, 0, unroll=2)
    power[...] = jnp.zeros_like(power)

    for g in range(4):
        for c, (_, rows, at) in enumerate(CHUNKS):
            if g < groups:
                if g == 0:
                    wait(recv[c].at[0 : BAND - 1], got.at[c])
                north, south = recv[c][0:16, g], recv[c][16:32, g]
            else:
                if g == groups:
                    wait(over[c].at[:, 0:3], hop2_got.at[c])
                block = over[c][:, :, g - groups].reshape(BAND, 4 * rows, 128)
                north, south = block[0:16], jnp.stack([block[BAND - 1 - d] for d in range(16)])
            for ref, block in ((xt_n, north), (xt_s, south)):
                for a, value in enumerate(quads(block) if rows == 4 else octets(block)):
                    ref[128 * a : 128 * a + 128, at : at + 16 * rows] = value
        for i in range(5):
            s = 5 * g + i
            order = start + s
            both = jnp.concatenate([xt_n[96 * i : 96 * i + 96, :], xt_s[96 * i : 96 * i + 96, :]], axis=0)
            value = jnp.dot(both, lp[s], preferred_element_type=F32)
            sign = (1 - 2 * ((degree + order) & 1)).astype(F32)
            value = value[0:96] + sign * value[96:192]
            first = jnp.where(s < count, order, NN)
            value = jnp.where(degree >= first, value, 0.0)
            spec[s] = value
            weight = jnp.where(order == 0, 1.0, 2.0).astype(F32)
            re, im = value[0:48], value[48:96]
            power[:, 0:NN] += weight * (re * re + im * im)
        pltpu.make_async_copy(spec.at[5 * g : 5 * g + 5], spec_ref.at[5 * g : 5 * g + 5], spec_sem.at[g]).start()

    for j in range(18):
        pieces[j] = power[8 * (j // 3) : 8 * (j // 3) + 8, 128 * (j % 3) : 128 * (j % 3) + 128]

    def spread(i, carry):
        peer = peer_of(i)

        @pl.when(peer < 18)
        def _():
            pltpu.make_async_remote_copy(
                src_ref=pieces.at[peer], dst_ref=parts.at[me], send_sem=power_send, recv_sem=power_recv,
                device_id={"band": peer}, device_id_type=MESH,
            ).start()
        return carry

    lax.fori_loop(0, BAND - 1, spread, 0)

    @pl.when(me < 18)
    def _():
        parts[me] = pieces[me]
        others = parts.at[0 : BAND - 1]
        wait(others, power_recv)
        column = 128 * lax.rem(me, 3) + lax.broadcasted_iota(jnp.int32, (8, 128), 1)
        value = jnp.sum(parts[...], axis=0) / (2 * column + 1).astype(F32)
        result[...] = value
        final[me] = value

        def share(i, carry):
            pltpu.make_async_remote_copy(
                src_ref=result, dst_ref=final.at[me], send_sem=final_send, recv_sem=final_recv,
                device_id={"band": peer_of(i)}, device_id_type=MESH,
            ).start()
            return carry

        lax.fori_loop(0, BAND - 1, share, 0)
        wait(final.at[0:17], final_recv)
        wait(others, final_send)
        wait(pieces.at[0:17], power_send)

    @pl.when(me >= 18)
    def _():
        wait(final, final_recv)
        wait(pieces, power_send)

    for j in range(18):
        g, t = j // 3, j % 3
        width = 128 if t < 2 else 64
        energy_ref[8 * g : 8 * g + 8, 128 * t : 128 * t + width] = final[j][:, :width]

    for c in range(3):
        wait(send[c].at[0 : BAND - 1], sent.at[c])
        if short:
            wait(over[c].at[0:7, 0], hop1_sent.at[c])
            wait(over[c].at[:, 0:3], hop2_sent.at[c])
    for g in range(4):
        pltpu.make_async_copy(spec.at[5 * g : 5 * g + 5], spec_ref.at[5 * g : 5 * g + 5], spec_sem.at[g]).wait()


def fused(short, starts, row_latitude, row_points, rows, legendre, pick):
    groups = 2 if short else 4
    smem = pl.BlockSpec(memory_space=pltpu.SMEM)
    vmem = pl.BlockSpec(memory_space=pltpu.VMEM)
    hbm = pl.BlockSpec(memory_space=pl.ANY)
    dma = pltpu.SemaphoreType.DMA
    return pl.pallas_call(
        functools.partial(fused_kernel, short),
        in_specs=[smem, smem, smem, hbm, hbm, vmem],
        out_specs=[hbm, vmem],
        out_shape=[
            jax.ShapeDtypeStruct((CAP, 2 * F, NN), F32),
            jax.ShapeDtypeStruct((F, NN), F32),
        ],
        scratch_shapes=[
            pltpu.VMEM((ROWS, F, 1280), F32),
            pltpu.VMEM((10, F, 128), F32),
            pltpu.VMEM((CAP, NN, NLATH), BF16),
            pltpu.VMEM((768, 256), BF16),
            pltpu.VMEM((384, 768), BF16),
            pltpu.VMEM((384, 768), BF16),
            pltpu.VMEM((LT, 8, 128), F32),
            *[pltpu.VMEM((BAND, groups, 4 * rows, 128), BF16) for _, rows, _ in CHUNKS * 2],
            *[pltpu.VMEM((8, 4, 2, 4 * rows, 128), BF16) for _, rows, _ in CHUNKS],
            pltpu.VMEM((CAP, NLATH, NN), BF16),
            pltpu.VMEM((512, NLATH), BF16),
            pltpu.VMEM((512, NLATH), BF16),
            pltpu.VMEM((CAP, 2 * F, NN), F32),
            pltpu.VMEM((F, 384), F32),
            pltpu.VMEM((18, 8, 128), F32),
            pltpu.VMEM((BAND, 8, 128), F32),
            pltpu.VMEM((8, 128), F32),
            pltpu.VMEM((18, 8, 128), F32),
            dma((ROWS,)), dma, dma((4,)),
            dma((3,)), dma((3,)), dma((3,)), dma((3,)), dma((3,)), dma((3,)),
            dma, dma, dma, dma,
        ],
        compiler_params=pltpu.CompilerParams(
            collective_id=0 if short else 1, has_side_effects=True, vmem_limit_bytes=VMEM
        ),
        name="short" if short else "full",
    )(starts, row_latitude, row_points, rows, legendre, pick)


def on_device(grid, row_points, row_latitude, order_owner, legendre):
    bands = jnp.arange(BAND + 1, dtype=jnp.int32)
    starts = jnp.sum((order_owner[None, :] < bands[:, None]).astype(jnp.int32), axis=1)
    crowded = starts[1:] - starts[:-1] > SHORT
    few = jnp.sum(crowded.astype(jnp.int32)) <= 1
    northern = row_latitude[:NLATH].reshape(BAND // 2, ROWS)
    ordered = sorted(CHUNKS, key=lambda chunk: chunk[2])
    column = jnp.concatenate([northern[:, first : first + rows].reshape(-1) for first, rows, _ in ordered])
    pick = (column[:, None] == jnp.arange(NLATH, dtype=jnp.int32)[None, :]).astype(BF16)
    rows = jnp.transpose(grid, (1, 0, 2))
    spectral, energy = lax.cond(
        few, functools.partial(fused, True), functools.partial(fused, False),
        starts, row_latitude, row_points, rows, legendre, pick,
    )
    return spectral.reshape(CAP, 2, F, NN), energy


def solution(mesh):
    in_specs = (P("member", "band", None), P(), P(), P(), P("band", None, None))
    out_specs = (P("band", None, "member", None), P("member", None))
    return jax.shard_map(
        on_device, mesh=mesh, in_specs=in_specs, out_specs=out_specs, check_vma=False
    )
```

```python
import functools
import math

import jax
import jax.numpy as jnp
from jax import lax
from jax.experimental import pallas as pl
from jax.experimental.pallas import tpu as pltpu
from jax.sharding import PartitionSpec as P

NN = 320
F = 48
ROWS = 20
CAP = 20
BAND = 32
NLATH = 320
SHORT = 10
LT = 248
VMEM = 56 * 1024 * 1024
MESH = pl.DeviceIdType.MESH
F32 = jnp.float32
BF16 = jnp.bfloat16


def cos_sin(turns):
    x = (turns - jnp.floor(turns + 0.5)) * (2.0 * math.pi)
    y = x * x
    c = jnp.full_like(x, 1.0 / math.factorial(20))
    for n in range(18, -2, -2):
        c = 1.0 / math.factorial(n) - c * y
    s = jnp.full_like(x, 1.0 / math.factorial(21))
    for n in range(19, -1, -2):
        s = 1.0 / math.factorial(n) - s * y
    return c, s * x


def cmul(a, b):
    return a[0] * b[0] - a[1] * b[1], a[0] * b[1] + a[1] * b[0]


def split(x):
    hi = x.astype(BF16)
    return hi, (x - hi.astype(F32)).astype(BF16)


def dft_row(x_ref, tile_ref, r, length, w_ref, b_ref, f_ref, slot):
    quarter = length // 4
    for t in range(10):
        tile_ref[t] = x_ref[r, :, 128 * t : 128 * t + 128]

    qf = jnp.full((8, 128), quarter, jnp.int32).astype(F32)
    inv_q = 1.0 / qf
    inv_l = 0.25 * inv_q
    sub = lax.broadcasted_iota(jnp.int32, (8, 128), 0)
    lane = lax.broadcasted_iota(jnp.int32, (8, 128), 1)

    def turns_of(count):
        num = count.astype(F32)
        return (num - jnp.floor(num * inv_q) * qf) * inv_q

    step = cos_sin(turns_of(8 * lane))
    tiles = [cos_sin(turns_of(sub * lane))]
    while len(tiles) < 48:
        room = 48 - len(tiles)
        tiles = tiles + [cmul(t, step) for t in tiles[:room]]
        step = cmul(step, step)
    for a in range(0, 48, 2):
        rows = 8 * a + lax.broadcasted_iota(jnp.int32, (16, 128), 0)
        scale = jnp.where(rows < quarter, jnp.concatenate([inv_l, inv_l], axis=0), 0.0)
        for part in range(2):
            value = jnp.concatenate([tiles[a][part], tiles[a + 1][part]], axis=0) * scale
            hi, lo = split(value)
            for at, piece in ((8 * a, hi), (384 + 8 * a, lo), (768 + 8 * a, hi)):
                w_ref[at : at + 16, 128 * part : 128 * part + 128] = piece

    psub = lax.broadcasted_iota(jnp.int32, (8, 384), 0)
    plane = lax.broadcasted_iota(jnp.int32, (8, 384), 1)
    lf = jnp.full((8, 384), length, jnp.int32).astype(F32)
    tc, ts = cos_sin((psub * plane).astype(F32) / lf)

    lane48 = lax.broadcasted_iota(jnp.int32, (F, 128), 1)

    def window(q):
        offset = q * quarter
        tile = offset >> 7
        rest = offset & 127
        parts = []
        for b in range(4):
            parts.append(pltpu.roll(tile_ref[jnp.minimum(tile + b, 9)], (128 - rest) & 127, axis=1))
        here = lane48 < 128 - rest
        return [jnp.where(here, parts[b], parts[b + 1]) for b in range(3)]

    w1, w2, w3 = window(1), window(2), window(3)
    for b in range(3):
        lo_at, hi_at = 128 * b, 128 * b + 128
        x0 = x_ref[r, :, lo_at:hi_at]
        e0, o0 = x0 + w2[b], x0 - w2[b]
        e1, o1 = w1[b] + w3[b], w1[b] - w3[b]
        c1, c2, c3 = (tc[p : p + 1, lo_at:hi_at] for p in (1, 2, 3))
        s1, s2, s3 = (ts[p : p + 1, lo_at:hi_at] for p in (1, 2, 3))
        y2 = e0 - e1
        pairs = [
            (e0 + e1, None),
            (o0 * c1 - o1 * s1, -(o0 * s1 + o1 * c1)),
            (y2 * c2, -(y2 * s2)),
            (o0 * c3 + o1 * s3, o1 * c3 - o0 * s3),
        ]
        row = 0
        for value in (v for pair in pairs for v in pair if v is not None):
            hi, lo = split(value)
            for at, piece in ((0, hi), (384, hi), (768, lo)):
                b_ref[row : row + 48, at + lo_at : at + hi_at] = piece
            row += 48

    sums = jnp.dot(b_ref[...], w_ref[...], preferred_element_type=F32)
    cosine = [sums[48 * i : 48 * i + 48, 0:128] for i in range(7)]
    sine = [sums[48 * i : 48 * i + 48, 128:256] for i in range(7)]
    blocks = [cosine[0], -sine[0]]
    for i in (1, 3, 5):
        blocks += [cosine[i] + sine[i + 1], cosine[i + 1] - sine[i]]
    total = jnp.concatenate(blocks, axis=0)
    for t in range(3):
        turned = total[128 * t : 128 * t + 128].T[:80]
        k = lax.broadcasted_iota(jnp.int32, (80, 128), 0)
        col = 128 * t + lax.broadcasted_iota(jnp.int32, (80, 128), 1)
        p = sum((col >= 96 * q).astype(jnp.int32) for q in (1, 2, 3))
        kept = jnp.where(4 * k + p < length // 2, turned, 0.0)
        f_ref[pl.ds(t, 80, stride=3), slot, :] = kept


def take_orders(f_ref, order):
    order = jnp.minimum(order, NN)
    rest = (96 * order) & 127
    tiles = f_ref[pl.ds((3 * order) >> 2, 5)].reshape(40, 128)
    rolled = pltpu.roll(tiles, (128 - rest) & 127, axis=1)
    here = lax.broadcasted_iota(jnp.int32, (8, 128), 1) < 128 - rest
    cut = [rolled[8 * j : 8 * j + 8] for j in range(5)]
    return [jnp.where(here, cut[j], cut[j + 1]) for j in range(4)]


def pack_eight(f_ref, order):
    return jnp.concatenate(take_orders(f_ref, order), axis=0).astype(BF16)


def pack_four(f_ref, order):
    v = take_orders(f_ref, order)
    low = lax.broadcasted_iota(jnp.int32, (8, 128), 0) < 4
    return jnp.concatenate(
        [jnp.where(low, v[j], pltpu.roll(v[j + 1], 4, axis=0)) for j in (0, 2)], axis=0
    ).astype(BF16)


def octets(block):
    wide = block.astype(F32).reshape(16, 4, 8, 128)
    return [wide[:, a].reshape(128, 128).T.astype(BF16) for a in range(4)]


def quads(block):
    wide = block.astype(F32).reshape(8, 2, 2, 8, 128)
    low = lax.broadcasted_iota(jnp.int32, (8, 8, 128), 1) < 4
    out = []
    for a in range(4):
        even, odd = wide[:, 0, a // 2], wide[:, 1, a // 2]
        if a % 2 == 0:
            tail = jnp.where(low, even, pltpu.roll(odd, 4, axis=1))
        else:
            tail = jnp.where(low, pltpu.roll(even, 4, axis=1), odd)
        out.append(tail.reshape(64, 128).T.astype(BF16))
    return out


def wait(ref, sem):
    pltpu.make_async_copy(ref, ref, sem).wait()


def far_first(i):
    a, b = i // 4, lax.rem(i, 4)
    dz = jnp.where(lax.rem(a, 2) == 1, 4 - (a + 1) // 2, 4 + a // 2)
    dy = jnp.where(lax.rem(b, 2) == 1, 2 - (b + 1) // 2, 2 + b // 2)
    return dz, dy


CHUNKS = ((0, 4, 256), (4, 8, 0), (12, 8, 128))


def fused_kernel(short, start_ref, lat_ref, points_ref, grid_ref, leg_hbm, pick_ref, spec_ref, energy_ref,
                 x_ref, tile_ref, leg_ref, w_ref, b_ref, f_ref,
                 send_0, send_1, send_2, recv_0, recv_1, recv_2, over_0, over_1, over_2,
                 lp, xt_n, xt_s, spec, power, pieces, parts, result, final,
                 x_sem, leg_sem, spec_sem, sent, got,
                 hop1_sent, hop1_got, hop2_sent, hop2_got,
                 power_send, power_recv, final_send, final_recv):
    groups = 2 if short else 4
    send, recv, over = (send_0, send_1, send_2), (recv_0, recv_1, recv_2), (over_0, over_1, over_2)
    me = lax.axis_index("band")
    z, y = me // 4, lax.rem(me, 4)
    place = jnp.where(me < 16, me, 47 - me)
    barrier = pltpu.get_barrier_semaphore()

    def greet(o, carry):
        pl.semaphore_signal(barrier, inc=1, device_id={"band": lax.rem(me + o, BAND)}, device_id_type=MESH)
        return carry

    def peer_of(i):
        dz, dy = far_first(i)
        return lax.rem(z + dz, 8) * 4 + lax.rem(y + dy, 4)

    def stored(r):
        return jnp.where(me < 16, r, ROWS - 1 - r)

    def load(r):
        return pltpu.make_async_copy(grid_ref.at[stored(r)], x_ref.at[r], x_sem.at[r])

    def load_row(r, carry):
        load(r).start()
        return carry

    lax.fori_loop(0, ROWS, load_row, 0)
    lax.fori_loop(1, BAND, greet, 0)
    leg_copy = pltpu.make_async_copy(leg_hbm, leg_ref, leg_sem)
    leg_copy.start()

    f_ref[240:] = jnp.zeros((8, 8, 128), F32)

    def crowd(d, carry):
        first = start_ref[d]
        return carry + jnp.where(start_ref[d + 1] - first > SHORT, first + SHORT, 0)

    extra = lax.fori_loop(0, BAND, crowd, 0) if short else None

    def dft_chunk(c):
        first, rows, _ = CHUNKS[c]

        def body(r, carry):
            load(r).wait()
            length = points_ref[lat_ref[me * ROWS + stored(r)]]
            dft_row(x_ref, tile_ref, r, length, w_ref, b_ref, f_ref, r - first)
            return carry

        lax.fori_loop(first, first + rows, body, 0)
        packer = pack_four if rows == 4 else pack_eight
        if short:
            for j in range(2):
                over[c][z, y, j] = packer(f_ref, extra + 5 * j)

        def pack(d, carry):
            for g in range(groups):
                send[c][d, g] = packer(f_ref, start_ref[d] + 5 * g)
            return carry

        lax.fori_loop(0, BAND, pack, 0, unroll=4)
        recv[c][place] = send[c][me]

    def send_chunk(c):
        if short:
            def hop1(o, carry):
                pltpu.make_async_remote_copy(
                    src_ref=over[c].at[z, y], dst_ref=over[c].at[z, y],
                    send_sem=hop1_sent.at[c], recv_sem=hop1_got.at[c],
                    device_id={"band": lax.rem(z + o, 8) * 4 + y}, device_id_type=MESH,
                ).start()
                return carry
            lax.fori_loop(1, 8, hop1, 0)

        def body(i, carry):
            peer = peer_of(i)
            pltpu.make_async_remote_copy(
                src_ref=send[c].at[peer], dst_ref=recv[c].at[place],
                send_sem=sent.at[c], recv_sem=got.at[c],
                device_id={"band": peer}, device_id_type=MESH,
            ).start()
            return carry

        lax.fori_loop(0, BAND - 1, body, 0, unroll=31)

    def forward(c):
        if not short:
            return
        wait(over[c].at[0:7, 0], hop1_got.at[c])

        def hop2(o, carry):
            pltpu.make_async_remote_copy(
                src_ref=over[c].at[:, y], dst_ref=over[c].at[:, y],
                send_sem=hop2_sent.at[c], recv_sem=hop2_got.at[c],
                device_id={"band": z * 4 + lax.rem(y + o, 4)}, device_id_type=MESH,
            ).start()
            return carry
        lax.fori_loop(1, 4, hop2, 0)

    dft_chunk(0)
    pl.semaphore_wait(barrier, BAND - 1)
    send_chunk(0)
    dft_chunk(1)
    send_chunk(1)
    forward(0)
    dft_chunk(2)
    send_chunk(2)
    leg_copy.wait()

    start = start_ref[me]
    count = start_ref[me + 1] - start
    degree = lax.broadcasted_iota(jnp.int32, (1, NN), 1)

    def permute(s, carry):
        lp[s] = lax.dot_general(
            pick_ref[...], leg_ref[s], (((1,), (1,)), ((), ())), preferred_element_type=F32
        ).astype(BF16)
        return carry

    lax.fori_loop(0, 2, permute, 0, unroll=2)
    forward(1)
    lax.fori_loop(2, SHORT, permute, 0, unroll=2)
    forward(2)
    lax.fori_loop(SHORT, CAP, permute, 0, unroll=2)
    power[...] = jnp.zeros_like(power)

    for g in range(4):
        for c, (_, rows, at) in enumerate(CHUNKS):
            if g < groups:
                if g == 0:
                    wait(recv[c].at[0 : BAND - 1], got.at[c])
                north, south = recv[c][0:16, g], recv[c][16:32, g]
            else:
                if g == groups:
                    wait(over[c].at[:, 0:3], hop2_got.at[c])
                block = over[c][:, :, g - groups].reshape(BAND, 4 * rows, 128)
                north, south = block[0:16], jnp.stack([block[BAND - 1 - d] for d in range(16)])
            for ref, block in ((xt_n, north), (xt_s, south)):
                for a, value in enumerate(quads(block) if rows == 4 else octets(block)):
                    ref[128 * a : 128 * a + 128, at : at + 16 * rows] = value
        for i in range(5):
            s = 5 * g + i
            order = start + s
            both = jnp.concatenate([xt_n[96 * i : 96 * i + 96, :], xt_s[96 * i : 96 * i + 96, :]], axis=0)
            value = jnp.dot(both, lp[s], preferred_element_type=F32)
            sign = (1 - 2 * ((degree + order) & 1)).astype(F32)
            value = value[0:96] + sign * value[96:192]
            first = jnp.where(s < count, order, NN)
            value = jnp.where(degree >= first, value, 0.0)
            spec[s] = value
            weight = jnp.where(order == 0, 1.0, 2.0).astype(F32)
            re, im = value[0:48], value[48:96]
            power[:, 0:NN] += weight * (re * re + im * im)
        pltpu.make_async_copy(spec.at[5 * g : 5 * g + 5], spec_ref.at[5 * g : 5 * g + 5], spec_sem.at[g]).start()

    for j in range(18):
        pieces[j] = power[8 * (j // 3) : 8 * (j // 3) + 8, 128 * (j % 3) : 128 * (j % 3) + 128]

    def spread(i, carry):
        peer = peer_of(i)

        @pl.when(peer < 18)
        def _():
            pltpu.make_async_remote_copy(
                src_ref=pieces.at[peer], dst_ref=parts.at[me], send_sem=power_send, recv_sem=power_recv,
                device_id={"band": peer}, device_id_type=MESH,
            ).start()
        return carry

    lax.fori_loop(0, BAND - 1, spread, 0, unroll=31)

    @pl.when(me < 18)
    def _():
        parts[me] = pieces[me]
        others = parts.at[0 : BAND - 1]
        wait(others, power_recv)
        column = 128 * lax.rem(me, 3) + lax.broadcasted_iota(jnp.int32, (8, 128), 1)
        value = jnp.sum(parts[...], axis=0) / (2 * column + 1).astype(F32)
        result[...] = value
        final[me] = value

        def share(i, carry):
            pltpu.make_async_remote_copy(
                src_ref=result, dst_ref=final.at[me], send_sem=final_send, recv_sem=final_recv,
                device_id={"band": peer_of(i)}, device_id_type=MESH,
            ).start()
            return carry

        lax.fori_loop(0, BAND - 1, share, 0, unroll=31)
        wait(final.at[0:17], final_recv)
        wait(others, final_send)
        wait(pieces.at[0:17], power_send)

    @pl.when(me >= 18)
    def _():
        wait(final, final_recv)
        wait(pieces, power_send)

    for j in range(18):
        g, t = j // 3, j % 3
        width = 128 if t < 2 else 64
        energy_ref[8 * g : 8 * g + 8, 128 * t : 128 * t + width] = final[j][:, :width]

    for c in range(3):
        wait(send[c].at[0 : BAND - 1], sent.at[c])
        if short:
            wait(over[c].at[0:7, 0], hop1_sent.at[c])
            wait(over[c].at[:, 0:3], hop2_sent.at[c])
    for g in range(4):
        pltpu.make_async_copy(spec.at[5 * g : 5 * g + 5], spec_ref.at[5 * g : 5 * g + 5], spec_sem.at[g]).wait()


def fused(short, starts, row_latitude, row_points, rows, legendre, pick):
    groups = 2 if short else 4
    smem = pl.BlockSpec(memory_space=pltpu.SMEM)
    vmem = pl.BlockSpec(memory_space=pltpu.VMEM)
    hbm = pl.BlockSpec(memory_space=pl.ANY)
    dma = pltpu.SemaphoreType.DMA
    return pl.pallas_call(
        functools.partial(fused_kernel, short),
        in_specs=[smem, smem, smem, hbm, hbm, vmem],
        out_specs=[hbm, vmem],
        out_shape=[
            jax.ShapeDtypeStruct((CAP, 2 * F, NN), F32),
            jax.ShapeDtypeStruct((F, NN), F32),
        ],
        scratch_shapes=[
            pltpu.VMEM((ROWS, F, 1280), F32),
            pltpu.VMEM((10, F, 128), F32),
            pltpu.VMEM((CAP, NN, NLATH), BF16),
            pltpu.VMEM((1152, 256), BF16),
            pltpu.VMEM((336, 1152), BF16),
            pltpu.VMEM((LT, 8, 128), F32),
            *[pltpu.VMEM((BAND, groups, 4 * rows, 128), BF16) for _, rows, _ in CHUNKS * 2],
            *[pltpu.VMEM((8, 4, 2, 4 * rows, 128), BF16) for _, rows, _ in CHUNKS],
            pltpu.VMEM((CAP, NLATH, NN), BF16),
            pltpu.VMEM((512, NLATH), BF16),
            pltpu.VMEM((512, NLATH), BF16),
            pltpu.VMEM((CAP, 2 * F, NN), F32),
            pltpu.VMEM((F, 384), F32),
            pltpu.VMEM((18, 8, 128), F32),
            pltpu.VMEM((BAND, 8, 128), F32),
            pltpu.VMEM((8, 128), F32),
            pltpu.VMEM((18, 8, 128), F32),
            dma((ROWS,)), dma, dma((4,)),
            dma((3,)), dma((3,)), dma((3,)), dma((3,)), dma((3,)), dma((3,)),
            dma, dma, dma, dma,
        ],
        compiler_params=pltpu.CompilerParams(
            collective_id=0 if short else 1, has_side_effects=True, vmem_limit_bytes=VMEM
        ),
        name="short" if short else "full",
    )(starts, row_latitude, row_points, rows, legendre, pick)


def on_device(grid, row_points, row_latitude, order_owner, legendre):
    bands = jnp.arange(BAND + 1, dtype=jnp.int32)
    starts = jnp.sum((order_owner[None, :] < bands[:, None]).astype(jnp.int32), axis=1)
    crowded = starts[1:] - starts[:-1] > SHORT
    few = jnp.sum(crowded.astype(jnp.int32)) <= 1
    northern = row_latitude[:NLATH].reshape(BAND // 2, ROWS)
    ordered = sorted(CHUNKS, key=lambda chunk: chunk[2])
    column = jnp.concatenate([northern[:, first : first + rows].reshape(-1) for first, rows, _ in ordered])
    pick = (column[:, None] == jnp.arange(NLATH, dtype=jnp.int32)[None, :]).astype(BF16)
    rows = jnp.transpose(grid, (1, 0, 2))
    spectral, energy = lax.cond(
        few, functools.partial(fused, True), functools.partial(fused, False),
        starts, row_latitude, row_points, rows, legendre, pick,
    )
    return spectral.reshape(CAP, 2, F, NN), energy


def solution(mesh):
    in_specs = (P("member", "band", None), P(), P(), P(), P("band", None, None))
    out_specs = (P("band", None, "member", None), P("member", None))
    return jax.shard_map(
        on_device, mesh=mesh, in_specs=in_specs, out_specs=out_specs, check_vma=False
    )
```
